32 devices in a mesh: row: 16 (over z, x, core), col: 2 (over y).
Axes of the slice: x: 2, y: 2, z: 4, core: 2. Of those that a mesh axis runs over, the one named last changes fastest.
Arguments:
- s_matrix: bfloat16 [2, 8192, 32768], P(None, 'row', 'col'), may hold values from -0.03125 to 0.03125
- slab: bfloat16 [2, 32768, 384], P(None, ('col', 'row')), may hold values from -6 to 6
- beam_hkl: int32 [3, 32768], P(None, ('col', 'row')), may hold values from -24 to 24
Outputs:
- squared: bfloat16 [2, 8192, 384], P(None, 'row', 'col')
The draws below stay inside these ranges and needn't reach their ends.
All inputs are finite; a program needn't handle non-finite values.
Results may differ from the reference program's by a relative error of at most 0.014.
Values may be sent and summed in bfloat16 or wider, within the bound.
No kernel may reach another device: no remote copies, remote signals or barrier semaphores. Data moves between devices by JAX's collectives and lax.ppermute only.
A program may use at most 128 MiB of HBM per device.

```python
import jax
import jax.numpy as jnp

N = 32768
C = 384
M = 8192


def set_ends(array, stream_key, least, largest):
    extent = array.shape
    index_at = [jax.random.randint(jax.random.fold_in(stream_key, axis), (), 0, extent[axis]) for axis in range(len(extent))]
    array = array.at[tuple(index_at)].set(least)
    longest = extent.index(max(extent))
    index_at[longest] = (index_at[longest] + 1) % extent[longest]
    return array.at[tuple(index_at)].set(largest)


def strengthened(drawn, rng, source, target, shards_of, factor):
    def block_of(axis_at):
        return (jnp.arange(drawn.shape[axis_at]) // (drawn.shape[axis_at] // shards_of)).reshape((-1,) + (1,) * (drawn.ndim - 1 - axis_at))

    one_side = jax.random.permutation(rng, shards_of)[block_of(target)]
    other_side = (block_of(target) + shards_of // 2) % shards_of
    return jnp.where((block_of(source) == one_side) | (block_of(source) == other_side), factor * drawn, drawn)


def steps_of(own_key, shape, shards, least, high):
    factor_of = 1.0
    for axis_at, blocks in shards:
        steps = jax.random.uniform(jax.random.fold_in(jax.random.fold_in(own_key, 6), axis_at), (blocks,), jnp.float32, least / len(shards), high / len(shards))
        factor_of = factor_of * jnp.repeat(jnp.exp(steps), shape[axis_at] // blocks).reshape((-1,) + (1,) * (len(shape) - 1 - axis_at))
    return factor_of


def gaussian(rng, extent, deviation, most, pieces=(), kind=jnp.bfloat16):
    result = deviation * jax.random.normal(rng, extent, jnp.float32)
    if pieces:
        result = result * steps_of(rng, extent, pieces, -0.22, 0.18)
    return jnp.clip(result, -most, most).astype(kind)


def heavy_noise(key, shape, width, most, pieces, heavy, dtype=jnp.bfloat16):
    array = width * jax.random.normal(key, shape, jnp.float32)
    if pieces:
        array = array * steps_of(key, shape, pieces, -0.22, 0.18)
    return jnp.clip(strengthened(array, jax.random.fold_in(key, 3), *heavy), -most, most).astype(dtype)


def setup_inputs(seed: int = 0) -> dict:
    key_list = jax.random.split(jax.random.key(seed), 4)
    return {
        "s_matrix": heavy_noise(key_list[0], (2, M, N), (2 * N) ** -0.5, 0.03125, ((1, 16), (2, 2)), (2, 1, 16, 2.0)),
        "slab": gaussian(key_list[1], (2, N, C), 1.0, 6.0, ((1, 32),)),
        "beam_hkl": set_ends(jax.random.randint(key_list[2], (3, N), -24, 25), jax.random.fold_in(key_list[2], 1), -24, 24).astype(jnp.int32),
    }


def reference(s_matrix, slab, beam_hkl):
    hkl_float = beam_hkl.astype(jnp.float32)
    angles = 0.61 * (hkl_float[0] * hkl_float[0] + hkl_float[1] * hkl_float[1] + hkl_float[2] * hkl_float[2]) + 0.29 * hkl_float[0] - 0.17 * hkl_float[1] + 0.43 * hkl_float[2]
    cosine = jnp.cos(angles)[:, None]
    sine = jnp.sin(angles)[:, None]
    slab_real = slab[0].astype(jnp.float32)
    slab_imag = slab[1].astype(jnp.float32)
    phased_real = (cosine * slab_real - sine * slab_imag).astype(jnp.bfloat16)
    phased_imag = (cosine * slab_imag + sine * slab_real).astype(jnp.bfloat16)
    part_real = jnp.dot(s_matrix[0], phased_real, preferred_element_type=jnp.float32) - jnp.dot(s_matrix[1], phased_imag, preferred_element_type=jnp.float32)
    part_imag = jnp.dot(s_matrix[0], phased_imag, preferred_element_type=jnp.float32) + jnp.dot(s_matrix[1], phased_real, preferred_element_type=jnp.float32)
    return jnp.stack([part_real, part_imag]).astype(jnp.bfloat16)
```

```python
import jax
import jax.numpy as jnp
import numpy as np
from jax import lax
from jax.experimental import pallas as pl
from jax.experimental.pallas import tpu as pltpu
from jax.sharding import PartitionSpec as P

PER_PLANE = 4
SLOTS = 4
IN_VMEM = pl.BlockSpec(memory_space=pltpu.VMEM)


def angles_of(hkl):
    h, k, l = (hkl[i : i + 1].astype(jnp.float32) for i in range(3))
    return 0.61 * (h * h + k * k + l * l) + 0.29 * h - 0.17 * k + 0.43 * l


def apply_phase(slab, beam_hkl):
    angles = angles_of(beam_hkl)
    cosine, sine = jnp.cos(angles), jnp.sin(angles)
    turned = jnp.swapaxes(slab, 1, 2).astype(jnp.float32)
    phased_real = cosine * turned[0] - sine * turned[1]
    phased_imag = cosine * turned[1] + sine * turned[0]
    return phased_real.astype(jnp.bfloat16), phased_imag.astype(jnp.bfloat16)


def phase_panels(slab, beam_hkl):
    _, depth, columns = slab.shape
    w = columns // 2

    def kernel(slab_ref, hkl_ref, whole_ref, first_ref, second_ref):
        col = lax.axis_index("col")
        angles = angles_of(hkl_ref[...])
        cosine, sine = jnp.cos(angles), jnp.sin(angles)
        row = lax.broadcasted_iota(jnp.int32, (columns, columns), 0)
        lane = lax.broadcasted_iota(jnp.int32, (columns, columns), 1)
        wanted = jnp.where(col == 0, jnp.where(row < w, row + w, row - w), row)
        select = jnp.where(lane == wanted, 1.0, 0.0).astype(jnp.bfloat16)

        def turned(part):
            return lax.dot_general(
                select, slab_ref[part], (((1,), (1,)), ((), ())), preferred_element_type=jnp.float32
            )

        real, imag = turned(0), turned(1)
        phased_real = (cosine * real - sine * imag).astype(jnp.bfloat16)
        phased_imag = (cosine * imag + sine * real).astype(jnp.bfloat16)
        for k, half_ref in enumerate((first_ref, second_ref)):
            rows = slice(k * w, (k + 1) * w)
            for j, phased in enumerate((phased_real, phased_imag)):
                half_ref[j * w : (j + 1) * w, :] = phased[rows]
                whole_ref[(2 * k + j) * w : (2 * k + j + 1) * w, :] = phased[rows]

    return pl.pallas_call(
        kernel,
        out_shape=[jax.ShapeDtypeStruct((n * columns, depth), jnp.bfloat16) for n in (2, 1, 1)],
        out_specs=[IN_VMEM] * 3,
        compiler_params=pltpu.CompilerParams(vmem_limit_bytes=34 * 2**20),
        cost_estimate=pl.CostEstimate(flops=1000, bytes_accessed=1000, transcendentals=0),
    )(slab, beam_hkl)


def after(value, *others):
    return lax.optimization_barrier((value,) + others)[0]


def multiply(which, blocks, s_matrix, pieces, total=None, finish=False, received=None):
    count = len(pieces)
    spans = [p[1:] if isinstance(p, tuple) else (0, p.shape[0]) for p in pieces]
    pieces = [p[0] if isinstance(p, tuple) else p for p in pieces]
    total_from = total[1] if isinstance(total, tuple) else 0
    in_place = total is not None and not isinstance(total, tuple) and not finish
    total = total[0] if isinstance(total, tuple) else total
    width, depth = spans[0][1], pieces[0].shape[1]
    rows = s_matrix.shape[1]
    half = width // 2
    extra = [v for v in (total, received) if v is not None]
    jobs = [(p, part) for p in range(count) for part in range(2)]
    slots = min(SLOTS, len(jobs))

    def kernel(blocks_ref, s_ref, *refs):
        piece_refs = refs[:count]
        total_ref = refs[count] if total is not None else None
        received_ref = refs[count + len(extra) - 1] if received is not None else None
        out_ref, held, arrived = refs[count + len(extra) : count + len(extra) + 3]
        sum_ref = refs[-1] if finish else out_ref

        def fetch(n):
            p, part = jobs[n]
            start = pl.multiple_of(blocks_ref[which[p]] * depth, depth)
            return pltpu.make_async_copy(
                s_ref.at[part, :, pl.ds(start, depth)], held.at[n % slots], arrived.at[n % slots]
            )

        for n in range(slots):
            fetch(n).start()
        for n, (p, part) in enumerate(jobs):
            fetch(n).wait()
            lanes = slice(part * rows, (part + 1) * rows)
            piece = piece_refs[p][spans[p][0] : spans[p][0] + width, :]
            product = lax.dot_general(
                piece, held[n % slots], (((1,), (1,)), ((), ())), preferred_element_type=jnp.float32
            )
            if p > 0:
                sum_ref[:, lanes] += product
            elif total is None:
                sum_ref[:, lanes] = product
            else:
                sum_ref[:, lanes] = total_ref[total_from : total_from + width, lanes] + product
            if n + slots < len(jobs):
                fetch(n + slots).start()
        if finish:
            real = sum_ref[:half, :rows] - sum_ref[half:, rows:]
            imag = sum_ref[half:, :rows] + sum_ref[:half, rows:]
            if received is not None:
                real += received_ref[0].astype(jnp.float32)
                imag += received_ref[1].astype(jnp.float32)
            out_ref[0] = real.astype(out_ref.dtype)
            out_ref[1] = imag.astype(out_ref.dtype)

    scratch = [pltpu.VMEM((slots, rows, depth), s_matrix.dtype), pltpu.SemaphoreType.DMA((slots,))]
    if finish:
        out_shape = jax.ShapeDtypeStruct((2, half, rows), jnp.bfloat16)
        scratch.append(pltpu.VMEM((width, 2 * rows), jnp.float32))
    else:
        out_shape = jax.ShapeDtypeStruct((width, 2 * rows), jnp.float32)
    return pl.pallas_call(
        kernel,
        out_shape=out_shape,
        in_specs=[pl.BlockSpec(memory_space=pltpu.SMEM), pl.BlockSpec(memory_space=pltpu.HBM)]
        + [IN_VMEM] * (count + len(extra)),
        out_specs=IN_VMEM,
        scratch_shapes=scratch,
        input_output_aliases={2 + count: 0} if in_place else {},
        compiler_params=pltpu.CompilerParams(vmem_limit_bytes=34 * 2**20),
        cost_estimate=pl.CostEstimate(flops=1000, bytes_accessed=1000, transcendentals=0),
    )(blocks, s_matrix, *pieces, *extra)


def choose(flag, first, second, row=0):
    rows = second.shape[0]

    def kernel(flag_ref, first_ref, second_ref, out_ref, done):
        del second_ref

        @pl.when(flag_ref[0] == 1)
        def _():
            copy = pltpu.make_async_copy(first_ref.at[row : row + rows, :], out_ref, done)
            copy.start()
            copy.wait()

    return pl.pallas_call(
        kernel,
        out_shape=jax.ShapeDtypeStruct(second.shape, second.dtype),
        in_specs=[pl.BlockSpec(memory_space=pltpu.SMEM)] + [pl.BlockSpec(memory_space=pl.ANY)] * 2,
        out_specs=pl.BlockSpec(memory_space=pl.ANY),
        scratch_shapes=[pltpu.SemaphoreType.DMA],
        input_output_aliases={2: 0},
        compiler_params=pltpu.CompilerParams(vmem_limit_bytes=34 * 2**20),
        cost_estimate=pl.CostEstimate(flops=1000, bytes_accessed=1000, transcendentals=0),
    )(flag, first, second)


def line_of_four(s_matrix, slab, beam_hkl):
    n_row = lax.axis_size("row")
    every = [(z, x, c) for z in range(n_row // PER_PLANE) for x in range(2) for c in range(2)]

    def index(z, x, c):
        return (z * 2 + x) * 2 + c

    def pairs(target, planes=(0, 1, 2, 3)):
        return [(index(*at), index(*target(*at))) for at in every if at[0] in planes]

    across = pairs(lambda z, x, c: (z, 1 - x, c))
    sibling = pairs(lambda z, x, c: (z, x, 1 - c))
    outer = pairs(lambda z, x, c: (z ^ 1, x, c))
    middle = pairs(lambda z, x, c: (3 - z, x, c), (1, 2))
    outward = pairs(lambda z, x, c: (z ^ 1, x, c), (1, 2))

    def send(value, route, what):
        with jax.named_scope("L_" + what):
            return lax.ppermute(value, "row", route)

    def far1(z):
        return 3 - z if z in (1, 2) else z ^ 2

    def far2(z):
        return z ^ 2 if z in (1, 2) else 3 - z

    me = lax.axis_index("row")
    held = {"O": lambda z: z, "P": lambda z: z ^ 1, "M": far1, "N": far2}
    names = [x + c + o for x in ("", "x") for c in ("", "c") for o in held]
    table = [
        [index(held[n[-1]](z), 1 - x if "x" in n else x, 1 - c if "c" in n else c) for n in names]
        + [int(z in (1, 2))]
        for z, x, c in every
    ]
    here = jnp.asarray(np.array(table, np.int32))[me]

    in_middle = here[len(names) :]
    O, Oa, Ob = phase_panels(slab, beam_hkl)
    wide = Oa.shape[0]

    def a(v):
        return (v, 0, wide)

    def b(v):
        return (v, wide, wide)

    def X(v, n):
        return send(v, across, "X" + n)

    def C(v, n):
        return send(v, sibling, "C" + n)

    def mul(which, pieces, total, **kw):
        return multiply([names.index(n) for n in which], here, s_matrix, pieces, total, **kw)

    ob = lax.optimization_barrier
    XO, P, Qa, Qb = X(O, "O"), send(O, outer, "P"), send(Oa, middle, "Qa"), send(Ob, middle, "Qb")
    CO = C(O, "O")
    AB = mul(["O", "cO"], [O, CO], None)
    Sa = send(Qa, outward, "Sa")
    P, Qb, XO, AB = ob((P, Qb, XO, AB))
    XPa, Sb, T = X(P[:wide], "Pa"), send(Qb, outward, "Sb"), send(P, middle, "T")
    CP, CXO = C(P, "P"), C(XO, "XO")
    AB = mul(["P", "xO"], [P, XO], AB)
    XPa, Sa, AB = ob((XPa, Sa, AB))
    M1a = choose(in_middle, Qa, Sa)
    XM1a = X(M1a, "M1a")
    CXPa, CM1a = C(XPa, "XPa"), C(M1a, "M1a")
    AB = mul(["cP", "xcO"], [CP, CXO], AB)
    A = mul(["xP", "M"], [XPa, M1a], a(AB))
    XM1a, T, Sb, A, AB = ob((XM1a, T, Sb, A, AB))
    M1b = choose(in_middle, Qb, Sb)
    XM1b = X(M1b, "M1b")
    Ua, Ub = send(T[:wide], outward, "Ua"), send(T[wide:], outward, "Ub")
    CXM1a, CM1b = C(XM1a, "XM1a"), C(M1b, "M1b")
    A = mul(["xcP", "cM", "xM"], [CXPa, CM1a, XM1a], A)
    XM1b, Ua, A = ob((XM1b, Ua, A))
    M2a = choose(in_middle, T, Ua)
    XM2a = X(M2a, "M2a")
    E = send(after(XO, Ua)[wide:], outer, "E")
    CXM1b, CM2a = C(XM1b, "XM1b"), C(M2a, "M2a")
    B = mul(["M", "cM", "xM"], [M1b, CM1b, XM1b], b(AB))
    A = mul(["N", "xcM"], [M2a, CXM1a], A)
    XM2a, Ub, A, B = ob((XM2a, Ub, A, B))
    M2b = choose(in_middle, T, Ub, wide)
    XM2b = X(M2b, "M2b")
    CXM2a, CM2b = C(XM2a, "XM2a"), C(M2b, "M2b")
    partial = mul(["cN", "xN", "xcN"], [CM2a, XM2a, CXM2a], A, finish=True)
    with jax.named_scope("L_partial"):
        received = lax.ppermute(partial, "col", [(0, 1), (1, 0)])
    B = mul(["xcM", "N"], [CXM1b, M2b], B)
    XM2b, E, B, received = ob((XM2b, E, B, received))
    CXM2b, CE = C(XM2b, "XM2b"), C(E, "E")
    B = mul(["cN", "xN", "xP"], [CM2b, XM2b, E], B)
    out = mul(["xcN", "xcP"], [CXM2b, CE], B, finish=True, received=received)
    return jnp.swapaxes(out, 1, 2)


def any_mesh(s_matrix, slab, beam_hkl):
    real, imag = apply_phase(slab, beam_hkl)
    gathered = lax.all_gather(jnp.stack([real, imag]), "row", axis=2, tiled=True)

    def dot(s, x):
        return lax.dot_general(x, s, (((1,), (1,)), ((), ())), preferred_element_type=jnp.float32)

    part_real = dot(s_matrix[0], gathered[0]) - dot(s_matrix[1], gathered[1])
    part_imag = dot(s_matrix[0], gathered[1]) + dot(s_matrix[1], gathered[0])
    totals = jnp.stack([part_real, part_imag]).astype(jnp.bfloat16)
    return jnp.swapaxes(lax.psum_scatter(totals, "col", scatter_dimension=1, tiled=True), 1, 2)


def solution(mesh):
    placed = (P(None, "row", "col"), P(None, ("col", "row"), None), P(None, ("col", "row")))
    line = mesh.shape["row"] == 4 * PER_PLANE and mesh.shape["col"] == 2
    return jax.shard_map(
        line_of_four if line else any_mesh,
        mesh=mesh,
        in_specs=placed,
        out_specs=P(None, "row", "col"),
        check_vma=False,
    )
```

```python
import jax
import jax.numpy as jnp
import numpy as np
from jax import lax
from jax.experimental import pallas as pl
from jax.experimental.pallas import tpu as pltpu
from jax.sharding import PartitionSpec as P

PER_PLANE = 4
SLOTS = 4
IN_VMEM = pl.BlockSpec(memory_space=pltpu.VMEM)


def angles_of(hkl):
    h, k, l = (hkl[i : i + 1].astype(jnp.float32) for i in range(3))
    return 0.61 * (h * h + k * k + l * l) + 0.29 * h - 0.17 * k + 0.43 * l


def apply_phase(slab, beam_hkl):
    angles = angles_of(beam_hkl)
    cosine, sine = jnp.cos(angles), jnp.sin(angles)
    turned = jnp.swapaxes(slab, 1, 2).astype(jnp.float32)
    phased_real = cosine * turned[0] - sine * turned[1]
    phased_imag = cosine * turned[1] + sine * turned[0]
    return phased_real.astype(jnp.bfloat16), phased_imag.astype(jnp.bfloat16)


def phase_panels(slab, beam_hkl):
    _, depth, columns = slab.shape
    w = columns // 2

    def kernel(slab_ref, hkl_ref, whole_ref, first_ref, second_ref):
        col = lax.axis_index("col")
        angles = angles_of(hkl_ref[...])
        cosine, sine = jnp.cos(angles), jnp.sin(angles)
        row = lax.broadcasted_iota(jnp.int32, (columns, columns), 0)
        lane = lax.broadcasted_iota(jnp.int32, (columns, columns), 1)
        wanted = jnp.where(col == 0, jnp.where(row < w, row + w, row - w), row)
        select = jnp.where(lane == wanted, 1.0, 0.0).astype(jnp.bfloat16)

        def turned(part):
            return lax.dot_general(
                select, slab_ref[part], (((1,), (1,)), ((), ())), preferred_element_type=jnp.float32
            )

        real, imag = turned(0), turned(1)
        phased_real = (cosine * real - sine * imag).astype(jnp.bfloat16)
        phased_imag = (cosine * imag + sine * real).astype(jnp.bfloat16)
        for k, half_ref in enumerate((first_ref, second_ref)):
            rows = slice(k * w, (k + 1) * w)
            for j, phased in enumerate((phased_real, phased_imag)):
                half_ref[j * w : (j + 1) * w, :] = phased[rows]
                whole_ref[(2 * k + j) * w : (2 * k + j + 1) * w, :] = phased[rows]

    return pl.pallas_call(
        kernel,
        out_shape=[jax.ShapeDtypeStruct((n * columns, depth), jnp.bfloat16) for n in (2, 1, 1)],
        out_specs=[IN_VMEM] * 3,
        compiler_params=pltpu.CompilerParams(vmem_limit_bytes=60 * 2**20),
        cost_estimate=pl.CostEstimate(flops=1000, bytes_accessed=1000, transcendentals=0),
    )(slab, beam_hkl)


def after(value, *others):
    return lax.optimization_barrier((value,) + others)[0]


def multiply(which, blocks, s_matrix, pieces, total=None, finish=False, received=None):
    count = len(pieces)
    spans = [p[1:] if isinstance(p, tuple) else (0, p.shape[0]) for p in pieces]
    pieces = [p[0] if isinstance(p, tuple) else p for p in pieces]
    total_from = total[1] if isinstance(total, tuple) else 0
    in_place = total is not None and not isinstance(total, tuple) and not finish
    total = total[0] if isinstance(total, tuple) else total
    width, depth = spans[0][1], pieces[0].shape[1]
    rows = s_matrix.shape[1]
    half = width // 2
    extra = [v for v in (total, received) if v is not None]
    jobs = [(p, part) for p in range(count) for part in range(2)]
    slots = min(SLOTS, len(jobs))

    def kernel(blocks_ref, s_ref, *refs):
        piece_refs = refs[:count]
        total_ref = refs[count] if total is not None else None
        received_ref = refs[count + len(extra) - 1] if received is not None else None
        out_ref, held, arrived = refs[count + len(extra) : count + len(extra) + 3]
        sum_ref = refs[-1] if finish else out_ref

        def fetch(n):
            p, part = jobs[n]
            start = pl.multiple_of(blocks_ref[which[p]] * depth, depth)
            return pltpu.make_async_copy(
                s_ref.at[part, :, pl.ds(start, depth)], held.at[n % slots], arrived.at[n % slots]
            )

        for n in range(slots):
            fetch(n).start()
        for n, (p, part) in enumerate(jobs):
            fetch(n).wait()
            lanes = slice(part * rows, (part + 1) * rows)
            piece = piece_refs[p][spans[p][0] : spans[p][0] + width, :]
            product = lax.dot_general(
                piece, held[n % slots], (((1,), (1,)), ((), ())), preferred_element_type=jnp.float32
            )
            if p > 0:
                sum_ref[:, lanes] += product
            elif total is None:
                sum_ref[:, lanes] = product
            else:
                sum_ref[:, lanes] = total_ref[total_from : total_from + width, lanes] + product
            if n + slots < len(jobs):
                fetch(n + slots).start()
        if finish:
            real = sum_ref[:half, :rows] - sum_ref[half:, rows:]
            imag = sum_ref[half:, :rows] + sum_ref[:half, rows:]
            if received is not None:
                real += received_ref[0].astype(jnp.float32)
                imag += received_ref[1].astype(jnp.float32)
            out_ref[0] = real.astype(out_ref.dtype)
            out_ref[1] = imag.astype(out_ref.dtype)

    scratch = [pltpu.VMEM((slots, rows, depth), s_matrix.dtype), pltpu.SemaphoreType.DMA((slots,))]
    if finish:
        out_shape = jax.ShapeDtypeStruct((2, half, rows), jnp.bfloat16)
        scratch.append(pltpu.VMEM((width, 2 * rows), jnp.float32))
    else:
        out_shape = jax.ShapeDtypeStruct((width, 2 * rows), jnp.float32)
    return pl.pallas_call(
        kernel,
        out_shape=out_shape,
        in_specs=[pl.BlockSpec(memory_space=pltpu.SMEM), pl.BlockSpec(memory_space=pltpu.HBM)]
        + [IN_VMEM] * (count + len(extra)),
        out_specs=IN_VMEM,
        scratch_shapes=scratch,
        input_output_aliases={2 + count: 0} if in_place else {},
        compiler_params=pltpu.CompilerParams(vmem_limit_bytes=34 * 2**20),
        cost_estimate=pl.CostEstimate(flops=1000, bytes_accessed=1000, transcendentals=0),
    )(blocks, s_matrix, *pieces, *extra)


def take(which, blocks, s_matrix, depth):
    rows = s_matrix.shape[1]

    def kernel(blocks_ref, s_ref, out_ref, done):
        copies = []
        for k, w in enumerate(which):
            start = pl.multiple_of(blocks_ref[w] * depth, depth)
            copies.append(pltpu.make_async_copy(s_ref.at[:, :, pl.ds(start, depth)], out_ref.at[k], done.at[k]))
        for copy in copies:
            copy.start()
        for copy in copies:
            copy.wait()

    return pl.pallas_call(
        kernel,
        out_shape=jax.ShapeDtypeStruct((len(which), 2, rows, depth), s_matrix.dtype),
        in_specs=[pl.BlockSpec(memory_space=pltpu.SMEM), pl.BlockSpec(memory_space=pltpu.HBM)],
        out_specs=IN_VMEM,
        scratch_shapes=[pltpu.SemaphoreType.DMA((len(which),))],
        compiler_params=pltpu.CompilerParams(vmem_limit_bytes=34 * 2**20),
        cost_estimate=pl.CostEstimate(flops=1000, bytes_accessed=1000, transcendentals=0),
    )(blocks, s_matrix)


def multiply_tiles(which, tiles, pieces, total, finish, received):
    count = len(pieces)
    width, depth = pieces[0].shape
    rows = tiles.shape[2]
    half = width // 2
    extra = [v for v in (total, received) if v is not None]

    def kernel(tiles_ref, *refs):
        total_ref = refs[count]
        received_ref = refs[count + 1] if received is not None else None
        out_ref = refs[count + len(extra)]
        sums = []
        for part in range(2):
            lanes = slice(part * rows, (part + 1) * rows)
            value = total_ref[:, lanes]
            for p in range(count):
                value += lax.dot_general(
                    refs[p][...], tiles_ref[which[p], part], (((1,), (1,)), ((), ())), preferred_element_type=jnp.float32
                )
            if finish:
                sums.append(value)
            else:
                out_ref[:, lanes] = value
        if finish:
            real = sums[0][:half] - sums[1][half:]
            imag = sums[0][half:] + sums[1][:half]
            if received is not None:
                real += received_ref[0].astype(jnp.float32)
                imag += received_ref[1].astype(jnp.float32)
            out_ref[0] = real.astype(out_ref.dtype)
            out_ref[1] = imag.astype(out_ref.dtype)

    out_shape = (
        jax.ShapeDtypeStruct((2, half, rows), jnp.bfloat16)
        if finish
        else jax.ShapeDtypeStruct((width, 2 * rows), jnp.float32)
    )
    return pl.pallas_call(
        kernel,
        out_shape=out_shape,
        in_specs=[IN_VMEM] * (1 + count + len(extra)),
        out_specs=IN_VMEM,
        input_output_aliases={} if finish else {1 + count: 0},
        compiler_params=pltpu.CompilerParams(vmem_limit_bytes=34 * 2**20),
        cost_estimate=pl.CostEstimate(flops=1000, bytes_accessed=1000, transcendentals=0),
    )(tiles, *pieces, *extra)


def choose(flag, first, second, row=0):
    rows = second.shape[0]

    def kernel(flag_ref, first_ref, second_ref, out_ref, done):
        del second_ref

        @pl.when(flag_ref[0] == 1)
        def _():
            copy = pltpu.make_async_copy(first_ref.at[row : row + rows, :], out_ref, done)
            copy.start()
            copy.wait()

    return pl.pallas_call(
        kernel,
        out_shape=jax.ShapeDtypeStruct(second.shape, second.dtype),
        in_specs=[pl.BlockSpec(memory_space=pltpu.SMEM)] + [pl.BlockSpec(memory_space=pl.ANY)] * 2,
        out_specs=pl.BlockSpec(memory_space=pl.ANY),
        scratch_shapes=[pltpu.SemaphoreType.DMA],
        input_output_aliases={2: 0},
        compiler_params=pltpu.CompilerParams(vmem_limit_bytes=34 * 2**20),
        cost_estimate=pl.CostEstimate(flops=1000, bytes_accessed=1000, transcendentals=0),
    )(flag, first, second)


def stack(*parts):
    offsets = [sum(v.shape[0] for v in parts[:k]) for k in range(len(parts))]

    def kernel(*refs):
        out_ref, done = refs[len(parts) :]
        copies = [
            pltpu.make_async_copy(refs[k], out_ref.at[offsets[k] : offsets[k] + v.shape[0], :], done.at[k])
            for k, v in enumerate(parts)
        ]
        for copy in copies:
            copy.start()
        for copy in copies:
            copy.wait()

    return pl.pallas_call(
        kernel,
        out_shape=jax.ShapeDtypeStruct((sum(v.shape[0] for v in parts), parts[0].shape[1]), parts[0].dtype),
        in_specs=[pl.BlockSpec(memory_space=pl.ANY)] * len(parts),
        out_specs=pl.BlockSpec(memory_space=pl.ANY),
        scratch_shapes=[pltpu.SemaphoreType.DMA((len(parts),))],
        compiler_params=pltpu.CompilerParams(vmem_limit_bytes=34 * 2**20),
        cost_estimate=pl.CostEstimate(flops=1000, bytes_accessed=1000, transcendentals=0),
    )(*parts)


def line_of_four(s_matrix, slab, beam_hkl):
    n_row = lax.axis_size("row")
    every = [(z, x, c) for z in range(n_row // PER_PLANE) for x in range(2) for c in range(2)]

    def index(z, x, c):
        return (z * 2 + x) * 2 + c

    def pairs(target, planes=(0, 1, 2, 3)):
        return [(index(*at), index(*target(*at))) for at in every if at[0] in planes]

    across = pairs(lambda z, x, c: (z, 1 - x, c))
    sibling = pairs(lambda z, x, c: (z, x, 1 - c))
    outer = pairs(lambda z, x, c: (z ^ 1, x, c))
    middle = pairs(lambda z, x, c: (3 - z, x, c), (1, 2))
    outward = pairs(lambda z, x, c: (z ^ 1, x, c), (1, 2))

    def send(value, route, what):
        with jax.named_scope("L_" + what):
            return lax.ppermute(value, "row", route)

    def far1(z):
        return 3 - z if z in (1, 2) else z ^ 2

    def far2(z):
        return z ^ 2 if z in (1, 2) else 3 - z

    me = lax.axis_index("row")
    held = {"O": lambda z: z, "P": lambda z: z ^ 1, "M": far1, "N": far2}
    names = [x + c + o for x in ("", "x") for c in ("", "c") for o in held]
    table = [
        [index(held[n[-1]](z), 1 - x if "x" in n else x, 1 - c if "c" in n else c) for n in names]
        + [int(z in (1, 2))]
        for z, x, c in every
    ]
    here = jnp.asarray(np.array(table, np.int32))[me]

    in_middle = here[len(names) :]
    O, Oa, Ob = phase_panels(slab, beam_hkl)
    wide = Oa.shape[0]

    def a(v):
        return (v, 0, wide)

    def b(v):
        return (v, wide, wide)

    def X(v, n):
        return send(v, across, "X" + n)

    def C(v, n):
        return send(v, sibling, "C" + n)

    def mul(which, pieces, total, **kw):
        return multiply([names.index(n) for n in which], here, s_matrix, pieces, total, **kw)

    ob = lax.optimization_barrier

    def upper(v):
        return (v, 0, v.shape[0] // 2)

    def lower(v):
        return (v, v.shape[0] // 2, v.shape[0] // 2)

    CO = C(O, "O")
    XO, Pa, Qa, Pb, Qb = (
        X(O, "O"), send(Oa, outer, "Pa"), send(Oa, middle, "Qa"), send(Ob, outer, "Pb"), send(Ob, middle, "Qb")
    )
    AB = mul(["O", "cO"], [O, CO], None)
    Pa, Qa = ob((Pa, Qa))
    Sa, Ta = send(Qa, outward, "Sa"), send(Pa, middle, "Ta")
    Pa, Pb, Qb, XO, AB = ob((Pa, Pb, Qb, XO, AB))
    XPa, Sb = X(Pa, "Pa"), send(Qb, outward, "Sb")
    CXO = C(XO, "XO")
    P = stack(Pa, Pb)
    AB = mul(["P", "xO"], [P, XO], AB)
    Sa, Ta, XPa, AB = ob((Sa, Ta, XPa, AB))
    M1a = choose(in_middle, Qa, Sa)
    XM1a = X(M1a, "M1a")
    Tb, Ua = send(after(Pb, Sa), middle, "Tb"), send(Ta, outward, "Ua")
    H = C(stack(XPa, M1a), "XPaM1a")
    AB = mul(["xcO"], [CXO], AB)
    A = mul(["xP", "M"], [XPa, M1a], a(AB))
    Sb, XM1a, A, AB = ob((Sb, XM1a, A, AB))
    M1b = choose(in_middle, Qb, Sb)
    XM1b = X(M1b, "M1b")
    Ub = send(Tb, outward, "Ub")
    CXM1a, CM1b = C(XM1a, "XM1a"), C(M1b, "M1b")
    A = mul(["xcP", "cM", "xM"], [upper(H), lower(H), XM1a], A)
    tiles = take([names.index(n) for n in ("xN", "xP", "xcN", "xcP")], after(here, A), s_matrix, O.shape[1])
    Ua, XM1b, XO, A = ob((Ua, XM1b, XO, A))
    M2a = choose(in_middle, Ta, Ua)
    XM2a = X(M2a, "M2a")
    E = send(XO[wide:], outer, "E")
    CXM1b, CM2a = C(XM1b, "XM1b"), C(M2a, "M2a")
    CPa = C(after(Pa, M2a), "Pa")
    A = mul(["N", "xcM"], [M2a, CXM1a], A)
    B = mul(["M", "cM", "xM"], [M1b, CM1b, XM1b], b(AB))
    Ub, A, B, tiles = ob((Ub, A, B, tiles))
    M2b = choose(in_middle, Tb, Ub)
    XM2b = X(M2b, "M2b")
    XM2a, M2b = ob((XM2a, M2b))
    CXM2a, CM2b = C(XM2a, "XM2a"), C(M2b, "M2b")
    CPb = C(after(Pb, M2b), "Pb")
    partial = mul(["cN", "cP", "xN", "xcN"], [CM2a, CPa, XM2a, CXM2a], A, finish=True)
    with jax.named_scope("L_partial"):
        received = lax.ppermute(partial, "col", [(0, 1), (1, 0)])
    B = mul(["xcM", "cP", "N", "cN"], [CXM1b, CPb, M2b, CM2b], B)
    XM2b, E, B, received, tiles = ob((XM2b, E, B, received, tiles))
    CXM2b, CE = C(XM2b, "XM2b"), C(E, "E")
    B = multiply_tiles([0, 1], tiles, [XM2b, E], B, False, None)
    out = multiply_tiles([2, 3], tiles, [CXM2b, CE], B, True, received)
    return jnp.swapaxes(out, 1, 2)


def any_mesh(s_matrix, slab, beam_hkl):
    real, imag = apply_phase(slab, beam_hkl)
    gathered = lax.all_gather(jnp.stack([real, imag]), "row", axis=2, tiled=True)

    def dot(s, x):
        return lax.dot_general(x, s, (((1,), (1,)), ((), ())), preferred_element_type=jnp.float32)

    part_real = dot(s_matrix[0], gathered[0]) - dot(s_matrix[1], gathered[1])
    part_imag = dot(s_matrix[0], gathered[1]) + dot(s_matrix[1], gathered[0])
    totals = jnp.stack([part_real, part_imag]).astype(jnp.bfloat16)
    return jnp.swapaxes(lax.psum_scatter(totals, "col", scatter_dimension=1, tiled=True), 1, 2)


def solution(mesh):
    placed = (P(None, "row", "col"), P(None, ("col", "row"), None), P(None, ("col", "row")))
    line = mesh.shape["row"] == 4 * PER_PLANE and mesh.shape["col"] == 2
    return jax.shard_map(
        line_of_four if line else any_mesh,
        mesh=mesh,
        in_specs=placed,
        out_specs=P(None, "row", "col"),
        check_vma=False,
    )
```

```python
import jax
import jax.numpy as jnp
import numpy as np
from jax import lax
from jax.experimental import pallas as pl
from jax.experimental.pallas import tpu as pltpu
from jax.sharding import PartitionSpec as P

PER_PLANE = 4
SLOTS = 4
IN_VMEM = pl.BlockSpec(memory_space=pltpu.VMEM)


def angles_of(hkl):
    h, k, l = (hkl[i : i + 1].astype(jnp.float32) for i in range(3))
    return 0.61 * (h * h + k * k + l * l) + 0.29 * h - 0.17 * k + 0.43 * l


def apply_phase(slab, beam_hkl):
    angles = angles_of(beam_hkl)
    cosine, sine = jnp.cos(angles), jnp.sin(angles)
    turned = jnp.swapaxes(slab, 1, 2).astype(jnp.float32)
    phased_real = cosine * turned[0] - sine * turned[1]
    phased_imag = cosine * turned[1] + sine * turned[0]
    return phased_real.astype(jnp.bfloat16), phased_imag.astype(jnp.bfloat16)


def phase_panels(slab, beam_hkl):
    _, depth, columns = slab.shape
    w = columns // 2
    block = depth // 2 if depth % 256 == 0 else depth

    def kernel(slab_ref, hkl_ref, whole_ref, first_ref, second_ref):
        col = lax.axis_index("col")
        angles = angles_of(hkl_ref[...])
        cosine, sine = jnp.cos(angles), jnp.sin(angles)
        row = lax.broadcasted_iota(jnp.int32, (columns, columns), 0)
        lane = lax.broadcasted_iota(jnp.int32, (columns, columns), 1)
        wanted = jnp.where(col == 0, jnp.where(row < w, row + w, row - w), row)
        select = jnp.where(lane == wanted, 1.0, 0.0).astype(jnp.bfloat16)

        def turned(part):
            return lax.dot_general(
                select, slab_ref[part], (((1,), (1,)), ((), ())), preferred_element_type=jnp.float32
            )

        real, imag = turned(0), turned(1)
        phased_real = (cosine * real - sine * imag).astype(jnp.bfloat16)
        phased_imag = (cosine * imag + sine * real).astype(jnp.bfloat16)
        for k, half_ref in enumerate((first_ref, second_ref)):
            rows = slice(k * w, (k + 1) * w)
            for j, phased in enumerate((phased_real, phased_imag)):
                half_ref[j * w : (j + 1) * w, :] = phased[rows]
                whole_ref[(2 * k + j) * w : (2 * k + j + 1) * w, :] = phased[rows]

    return pl.pallas_call(
        kernel,
        out_shape=[jax.ShapeDtypeStruct((n * columns, depth), jnp.bfloat16) for n in (2, 1, 1)],
        grid=(depth // block,),
        in_specs=[
            pl.BlockSpec((2, block, columns), lambda i: (0, i, 0)),
            pl.BlockSpec((3, block), lambda i: (0, i)),
        ],
        out_specs=[pl.BlockSpec((n * columns, block), lambda i: (0, i)) for n in (2, 1, 1)],
        compiler_params=pltpu.CompilerParams(vmem_limit_bytes=60 * 2**20),
        cost_estimate=pl.CostEstimate(flops=1000, bytes_accessed=1000, transcendentals=0),
    )(slab, beam_hkl)


def after(value, *others):
    return lax.optimization_barrier((value,) + others)[0]


def multiply(which, blocks, s_matrix, pieces, total=None, finish=False, received=None):
    count = len(pieces)
    spans = [p[1:] if isinstance(p, tuple) else (0, p.shape[0]) for p in pieces]
    pieces = [p[0] if isinstance(p, tuple) else p for p in pieces]
    total_from = total[1] if isinstance(total, tuple) else 0
    in_place = total is not None and not isinstance(total, tuple) and not finish
    total = total[0] if isinstance(total, tuple) else total
    width, depth = spans[0][1], pieces[0].shape[1]
    rows = s_matrix.shape[1]
    half = width // 2
    extra = [v for v in (total, received) if v is not None]
    jobs = [(p, part) for p in range(count) for part in range(2)]
    slots = min(SLOTS, len(jobs))

    def kernel(blocks_ref, s_ref, *refs):
        piece_refs = refs[:count]
        total_ref = refs[count] if total is not None else None
        received_ref = refs[count + len(extra) - 1] if received is not None else None
        out_ref, held, arrived = refs[count + len(extra) : count + len(extra) + 3]
        sum_ref = refs[-1] if finish else out_ref

        def fetch(n):
            p, part = jobs[n]
            start = pl.multiple_of(blocks_ref[which[p]] * depth, depth)
            return pltpu.make_async_copy(
                s_ref.at[part, :, pl.ds(start, depth)], held.at[n % slots], arrived.at[n % slots]
            )

        for n in range(slots):
            fetch(n).start()
        for n, (p, part) in enumerate(jobs):
            fetch(n).wait()
            lanes = slice(part * rows, (part + 1) * rows)
            piece = piece_refs[p][spans[p][0] : spans[p][0] + width, :]
            product = lax.dot_general(
                piece, held[n % slots], (((1,), (1,)), ((), ())), preferred_element_type=jnp.float32
            )
            if p > 0:
                sum_ref[:, lanes] += product
            elif total is None:
                sum_ref[:, lanes] = product
            else:
                sum_ref[:, lanes] = total_ref[total_from : total_from + width, lanes] + product
            if n + slots < len(jobs):
                fetch(n + slots).start()
        if finish:
            real = sum_ref[:half, :rows] - sum_ref[half:, rows:]
            imag = sum_ref[half:, :rows] + sum_ref[:half, rows:]
            if received is not None:
                real += received_ref[0].astype(jnp.float32)
                imag += received_ref[1].astype(jnp.float32)
            out_ref[0] = real.astype(out_ref.dtype)
            out_ref[1] = imag.astype(out_ref.dtype)

    scratch = [pltpu.VMEM((slots, rows, depth), s_matrix.dtype), pltpu.SemaphoreType.DMA((slots,))]
    if finish:
        out_shape = jax.ShapeDtypeStruct((2, half, rows), jnp.bfloat16)
        scratch.append(pltpu.VMEM((width, 2 * rows), jnp.float32))
    else:
        out_shape = jax.ShapeDtypeStruct((width, 2 * rows), jnp.float32)
    return pl.pallas_call(
        kernel,
        out_shape=out_shape,
        in_specs=[pl.BlockSpec(memory_space=pltpu.SMEM), pl.BlockSpec(memory_space=pltpu.HBM)]
        + [IN_VMEM] * (count + len(extra)),
        out_specs=IN_VMEM,
        scratch_shapes=scratch,
        input_output_aliases={2 + count: 0} if in_place else {},
        compiler_params=pltpu.CompilerParams(vmem_limit_bytes=34 * 2**20),
        cost_estimate=pl.CostEstimate(flops=1000, bytes_accessed=1000, transcendentals=0),
    )(blocks, s_matrix, *pieces, *extra)


def take(which, blocks, s_matrix, depth):
    rows = s_matrix.shape[1]

    def kernel(blocks_ref, s_ref, out_ref, done):
        copies = []
        for k, w in enumerate(which):
            start = pl.multiple_of(blocks_ref[w] * depth, depth)
            copies.append(pltpu.make_async_copy(s_ref.at[:, :, pl.ds(start, depth)], out_ref.at[k], done.at[k]))
        for copy in copies:
            copy.start()
        for copy in copies:
            copy.wait()

    return pl.pallas_call(
        kernel,
        out_shape=jax.ShapeDtypeStruct((len(which), 2, rows, depth), s_matrix.dtype),
        in_specs=[pl.BlockSpec(memory_space=pltpu.SMEM), pl.BlockSpec(memory_space=pltpu.HBM)],
        out_specs=IN_VMEM,
        scratch_shapes=[pltpu.SemaphoreType.DMA((len(which),))],
        compiler_params=pltpu.CompilerParams(vmem_limit_bytes=34 * 2**20),
        cost_estimate=pl.CostEstimate(flops=1000, bytes_accessed=1000, transcendentals=0),
    )(blocks, s_matrix)


def multiply_tiles(which, tiles, pieces, total, finish, received):
    count = len(pieces)
    width, depth = pieces[0].shape
    rows = tiles.shape[2]
    half = width // 2
    extra = [v for v in (total, received) if v is not None]

    def kernel(tiles_ref, *refs):
        total_ref = refs[count]
        received_ref = refs[count + 1] if received is not None else None
        out_ref = refs[count + len(extra)]
        sums = []
        for part in range(2):
            lanes = slice(part * rows, (part + 1) * rows)
            value = total_ref[:, lanes]
            for p in range(count):
                value += lax.dot_general(
                    refs[p][...], tiles_ref[which[p], part], (((1,), (1,)), ((), ())), preferred_element_type=jnp.float32
                )
            if finish:
                sums.append(value)
            else:
                out_ref[:, lanes] = value
        if finish:
            real = sums[0][:half] - sums[1][half:]
            imag = sums[0][half:] + sums[1][:half]
            if received is not None:
                real += received_ref[0].astype(jnp.float32)
                imag += received_ref[1].astype(jnp.float32)
            out_ref[0] = real.astype(out_ref.dtype)
            out_ref[1] = imag.astype(out_ref.dtype)

    out_shape = (
        jax.ShapeDtypeStruct((2, half, rows), jnp.bfloat16)
        if finish
        else jax.ShapeDtypeStruct((width, 2 * rows), jnp.float32)
    )
    return pl.pallas_call(
        kernel,
        out_shape=out_shape,
        in_specs=[IN_VMEM] * (1 + count + len(extra)),
        out_specs=IN_VMEM,
        input_output_aliases={} if finish else {1 + count: 0},
        compiler_params=pltpu.CompilerParams(vmem_limit_bytes=34 * 2**20),
        cost_estimate=pl.CostEstimate(flops=1000, bytes_accessed=1000, transcendentals=0),
    )(tiles, *pieces, *extra)


def choose(flag, first, second, row=0):
    rows = second.shape[0]

    def kernel(flag_ref, first_ref, second_ref, out_ref, done):
        del second_ref

        @pl.when(flag_ref[0] == 1)
        def _():
            copy = pltpu.make_async_copy(first_ref.at[row : row + rows, :], out_ref, done)
            copy.start()
            copy.wait()

    return pl.pallas_call(
        kernel,
        out_shape=jax.ShapeDtypeStruct(second.shape, second.dtype),
        in_specs=[pl.BlockSpec(memory_space=pltpu.SMEM)] + [pl.BlockSpec(memory_space=pl.ANY)] * 2,
        out_specs=pl.BlockSpec(memory_space=pl.ANY),
        scratch_shapes=[pltpu.SemaphoreType.DMA],
        input_output_aliases={2: 0},
        compiler_params=pltpu.CompilerParams(vmem_limit_bytes=34 * 2**20),
        cost_estimate=pl.CostEstimate(flops=1000, bytes_accessed=1000, transcendentals=0),
    )(flag, first, second)


def stack(*parts):
    offsets = [sum(v.shape[0] for v in parts[:k]) for k in range(len(parts))]

    def kernel(*refs):
        out_ref, done = refs[len(parts) :]
        copies = [
            pltpu.make_async_copy(refs[k], out_ref.at[offsets[k] : offsets[k] + v.shape[0], :], done.at[k])
            for k, v in enumerate(parts)
        ]
        for copy in copies:
            copy.start()
        for copy in copies:
            copy.wait()

    return pl.pallas_call(
        kernel,
        out_shape=jax.ShapeDtypeStruct((sum(v.shape[0] for v in parts), parts[0].shape[1]), parts[0].dtype),
        in_specs=[pl.BlockSpec(memory_space=pl.ANY)] * len(parts),
        out_specs=pl.BlockSpec(memory_space=pl.ANY),
        scratch_shapes=[pltpu.SemaphoreType.DMA((len(parts),))],
        compiler_params=pltpu.CompilerParams(vmem_limit_bytes=34 * 2**20),
        cost_estimate=pl.CostEstimate(flops=1000, bytes_accessed=1000, transcendentals=0),
    )(*parts)


def line_of_four(s_matrix, slab, beam_hkl):
    n_row = lax.axis_size("row")
    every = [(z, x, c) for z in range(n_row // PER_PLANE) for x in range(2) for c in range(2)]

    def index(z, x, c):
        return (z * 2 + x) * 2 + c

    def pairs(target, planes=(0, 1, 2, 3)):
        return [(index(*at), index(*target(*at))) for at in every if at[0] in planes]

    across = pairs(lambda z, x, c: (z, 1 - x, c))
    sibling = pairs(lambda z, x, c: (z, x, 1 - c))
    outer = pairs(lambda z, x, c: (z ^ 1, x, c))
    middle = pairs(lambda z, x, c: (3 - z, x, c), (1, 2))
    outward = pairs(lambda z, x, c: (z ^ 1, x, c), (1, 2))

    def send(value, route, what):
        with jax.named_scope("L_" + what):
            return lax.ppermute(value, "row", route)

    def far1(z):
        return 3 - z if z in (1, 2) else z ^ 2

    def far2(z):
        return z ^ 2 if z in (1, 2) else 3 - z

    me = lax.axis_index("row")
    held = {"O": lambda z: z, "P": lambda z: z ^ 1, "M": far1, "N": far2}
    names = [x + c + o for x in ("", "x") for c in ("", "c") for o in held]
    table = [
        [index(held[n[-1]](z), 1 - x if "x" in n else x, 1 - c if "c" in n else c) for n in names]
        + [int(z in (1, 2))]
        for z, x, c in every
    ]
    here = jnp.asarray(np.array(table, np.int32))[me]

    in_middle = here[len(names) :]
    O, Oa, Ob = phase_panels(slab, beam_hkl)
    wide = Oa.shape[0]

    def a(v):
        return (v, 0, wide)

    def b(v):
        return (v, wide, wide)

    def X(v, n):
        return send(v, across, "X" + n)

    def C(v, n):
        return send(v, sibling, "C" + n)

    def mul(which, pieces, total, **kw):
        return multiply([names.index(n) for n in which], here, s_matrix, pieces, total, **kw)

    ob = lax.optimization_barrier

    def upper(v):
        return (v, 0, v.shape[0] // 2)

    def lower(v):
        return (v, v.shape[0] // 2, v.shape[0] // 2)

    CO = C(O, "O")
    XO, Pa, Qa, Pb, Qb = (
        X(O, "O"), send(Oa, outer, "Pa"), send(Oa, middle, "Qa"), send(Ob, outer, "Pb"), send(Ob, middle, "Qb")
    )
    AB = mul(["O", "cO"], [O, CO], None)
    Pa, Qa = ob((Pa, Qa))
    Sa, Ta = send(Qa, outward, "Sa"), send(Pa, middle, "Ta")
    Pa, Pb, Qb, XO, AB = ob((Pa, Pb, Qb, XO, AB))
    XPa, Sb = X(Pa, "Pa"), send(Qb, outward, "Sb")
    CXO = C(XO, "XO")
    P = stack(Pa, Pb)
    AB = mul(["P", "xO"], [P, XO], AB)
    Sa, Ta, XPa, AB = ob((Sa, Ta, XPa, AB))
    M1a = choose(in_middle, Qa, Sa)
    XM1a = X(M1a, "M1a")
    Tb, Ua = send(after(Pb, Sa), middle, "Tb"), send(Ta, outward, "Ua")
    H = C(stack(XPa, M1a), "XPaM1a")
    AB = mul(["xcO"], [CXO], AB)
    A = mul(["xP", "M"], [XPa, M1a], a(AB))
    Sb, XM1a, A, AB = ob((Sb, XM1a, A, AB))
    M1b = choose(in_middle, Qb, Sb)
    XM1b = X(M1b, "M1b")
    Ub = send(Tb, outward, "Ub")
    CXM1a, CM1b = C(XM1a, "XM1a"), C(M1b, "M1b")
    A = mul(["xcP", "cM", "xM"], [upper(H), lower(H), XM1a], A)
    tiles = take([names.index(n) for n in ("xN", "xP", "xcN", "xcP")], after(here, A), s_matrix, O.shape[1])
    Ua, XM1b, XO, A = ob((Ua, XM1b, XO, A))
    M2a = choose(in_middle, Ta, Ua)
    XM2a = X(M2a, "M2a")
    E = send(XO[wide:], outer, "E")
    CXM1b, CM2a = C(XM1b, "XM1b"), C(M2a, "M2a")
    CPa = C(after(Pa, M2a), "Pa")
    A = mul(["N", "xcM"], [M2a, CXM1a], A)
    B = mul(["M", "cM", "xM"], [M1b, CM1b, XM1b], b(AB))
    Ub, A, B, tiles = ob((Ub, A, B, tiles))
    M2b = choose(in_middle, Tb, Ub)
    XM2b = X(M2b, "M2b")
    XM2a, M2b = ob((XM2a, M2b))
    CXM2a, CM2b = C(XM2a, "XM2a"), C(M2b, "M2b")
    CPb = C(after(Pb, M2b), "Pb")
    partial = mul(["cN", "cP", "xN", "xcN"], [CM2a, CPa, XM2a, CXM2a], A, finish=True)
    with jax.named_scope("L_partial"):
        received = lax.ppermute(partial, "col", [(0, 1), (1, 0)])
    B = mul(["xcM", "cP", "N", "cN"], [CXM1b, CPb, M2b, CM2b], B)
    XM2b, E, B, received, tiles = ob((XM2b, E, B, received, tiles))
    CXM2b, CE = C(XM2b, "XM2b"), C(E, "E")
    B = multiply_tiles([0, 1], tiles, [XM2b, E], B, False, None)
    out = multiply_tiles([2, 3], tiles, [CXM2b, CE], B, True, received)
    return jnp.swapaxes(out, 1, 2)


def any_mesh(s_matrix, slab, beam_hkl):
    real, imag = apply_phase(slab, beam_hkl)
    gathered = lax.all_gather(jnp.stack([real, imag]), "row", axis=2, tiled=True)

    def dot(s, x):
        return lax.dot_general(x, s, (((1,), (1,)), ((), ())), preferred_element_type=jnp.float32)

    part_real = dot(s_matrix[0], gathered[0]) - dot(s_matrix[1], gathered[1])
    part_imag = dot(s_matrix[0], gathered[1]) + dot(s_matrix[1], gathered[0])
    totals = jnp.stack([part_real, part_imag]).astype(jnp.bfloat16)
    return jnp.swapaxes(lax.psum_scatter(totals, "col", scatter_dimension=1, tiled=True), 1, 2)


def solution(mesh):
    placed = (P(None, "row", "col"), P(None, ("col", "row"), None), P(None, ("col", "row")))
    line = mesh.shape["row"] == 4 * PER_PLANE and mesh.shape["col"] == 2
    return jax.shard_map(
        line_of_four if line else any_mesh,
        mesh=mesh,
        in_specs=placed,
        out_specs=P(None, "row", "col"),
        check_vma=False,
    )
```

```python
import jax
import jax.numpy as jnp
import numpy as np
from jax import lax
from jax.experimental import pallas as pl
from jax.experimental.pallas import tpu as pltpu
from jax.sharding import PartitionSpec as P

PER_PLANE = 4
SLOTS = 4
IN_VMEM = pl.BlockSpec(memory_space=pltpu.VMEM)


def angles_of(hkl):
    h, k, l = (hkl[i : i + 1].astype(jnp.float32) for i in range(3))
    return 0.61 * (h * h + k * k + l * l) + 0.29 * h - 0.17 * k + 0.43 * l


def apply_phase(slab, beam_hkl):
    angles = angles_of(beam_hkl)
    cosine, sine = jnp.cos(angles), jnp.sin(angles)
    turned = jnp.swapaxes(slab, 1, 2).astype(jnp.float32)
    phased_real = cosine * turned[0] - sine * turned[1]
    phased_imag = cosine * turned[1] + sine * turned[0]
    return phased_real.astype(jnp.bfloat16), phased_imag.astype(jnp.bfloat16)


def phase_panels(slab, beam_hkl):
    _, depth, columns = slab.shape
    w = columns // 2
    block = depth // 2 if depth % 256 == 0 else depth

    def kernel(slab_ref, hkl_ref, whole_ref, first_ref, second_ref):
        col = lax.axis_index("col")
        angles = angles_of(hkl_ref[...])
        cosine, sine = jnp.cos(angles), jnp.sin(angles)
        row = lax.broadcasted_iota(jnp.int32, (columns, columns), 0)
        lane = lax.broadcasted_iota(jnp.int32, (columns, columns), 1)
        wanted = jnp.where(col == 0, jnp.where(row < w, row + w, row - w), row)
        select = jnp.where(lane == wanted, 1.0, 0.0).astype(jnp.bfloat16)

        def turned(part):
            return lax.dot_general(
                select, slab_ref[part], (((1,), (1,)), ((), ())), preferred_element_type=jnp.float32
            )

        real, imag = turned(0), turned(1)
        phased_real = (cosine * real - sine * imag).astype(jnp.bfloat16)
        phased_imag = (cosine * imag + sine * real).astype(jnp.bfloat16)
        for k, half_ref in enumerate((first_ref, second_ref)):
            rows = slice(k * w, (k + 1) * w)
            for j, phased in enumerate((phased_real, phased_imag)):
                half_ref[j * w : (j + 1) * w, :] = phased[rows]
                whole_ref[(2 * k + j) * w : (2 * k + j + 1) * w, :] = phased[rows]

    return pl.pallas_call(
        kernel,
        out_shape=[jax.ShapeDtypeStruct((n * columns, depth), jnp.bfloat16) for n in (2, 1, 1)],
        grid=(depth // block,),
        in_specs=[
            pl.BlockSpec((2, block, columns), lambda i: (0, i, 0)),
            pl.BlockSpec((3, block), lambda i: (0, i)),
        ],
        out_specs=[pl.BlockSpec((n * columns, block), lambda i: (0, i)) for n in (2, 1, 1)],
        compiler_params=pltpu.CompilerParams(vmem_limit_bytes=60 * 2**20),
        cost_estimate=pl.CostEstimate(flops=1000, bytes_accessed=1000, transcendentals=0),
    )(slab, beam_hkl)


def after(value, *others):
    return lax.optimization_barrier((value,) + others)[0]


def multiply(which, blocks, s_matrix, pieces, total=None, finish=False, received=None):
    count = len(pieces)
    spans = [p[1:] if isinstance(p, tuple) else (0, p.shape[0]) for p in pieces]
    pieces = [p[0] if isinstance(p, tuple) else p for p in pieces]
    total_from = total[1] if isinstance(total, tuple) else 0
    in_place = total is not None and not isinstance(total, tuple) and not finish
    total = total[0] if isinstance(total, tuple) else total
    width, depth = spans[0][1], pieces[0].shape[1]
    rows = s_matrix.shape[1]
    half = width // 2
    extra = [v for v in (total, received) if v is not None]
    jobs = [(p, part) for p in range(count) for part in range(2)]
    slots = min(SLOTS, len(jobs))

    def kernel(blocks_ref, s_ref, *refs):
        piece_refs = refs[:count]
        total_ref = refs[count] if total is not None else None
        received_ref = refs[count + len(extra) - 1] if received is not None else None
        out_ref, held, arrived = refs[count + len(extra) : count + len(extra) + 3]
        sum_ref = refs[-1] if finish else out_ref

        def fetch(n):
            p, part = jobs[n]
            start = pl.multiple_of(blocks_ref[which[p]] * depth, depth)
            return pltpu.make_async_copy(
                s_ref.at[part, :, pl.ds(start, depth)], held.at[n % slots], arrived.at[n % slots]
            )

        for n in range(slots):
            fetch(n).start()
        for n, (p, part) in enumerate(jobs):
            fetch(n).wait()
            lanes = slice(part * rows, (part + 1) * rows)
            piece = piece_refs[p][spans[p][0] : spans[p][0] + width, :]
            product = lax.dot_general(
                piece, held[n % slots], (((1,), (1,)), ((), ())), preferred_element_type=jnp.float32
            )
            if p > 0:
                sum_ref[:, lanes] += product
            elif total is None:
                sum_ref[:, lanes] = product
            else:
                sum_ref[:, lanes] = total_ref[total_from : total_from + width, lanes] + product
            if n + slots < len(jobs):
                fetch(n + slots).start()
        if finish:
            real = sum_ref[:half, :rows] - sum_ref[half:, rows:]
            imag = sum_ref[half:, :rows] + sum_ref[:half, rows:]
            if received is not None:
                real += received_ref[0].astype(jnp.float32)
                imag += received_ref[1].astype(jnp.float32)
            out_ref[0] = real.astype(out_ref.dtype)
            out_ref[1] = imag.astype(out_ref.dtype)

    scratch = [pltpu.VMEM((slots, rows, depth), s_matrix.dtype), pltpu.SemaphoreType.DMA((slots,))]
    if finish:
        out_shape = jax.ShapeDtypeStruct((2, half, rows), jnp.bfloat16)
        scratch.append(pltpu.VMEM((width, 2 * rows), jnp.float32))
    else:
        out_shape = jax.ShapeDtypeStruct((width, 2 * rows), jnp.float32)
    return pl.pallas_call(
        kernel,
        out_shape=out_shape,
        in_specs=[pl.BlockSpec(memory_space=pltpu.SMEM), pl.BlockSpec(memory_space=pltpu.HBM)]
        + [IN_VMEM] * (count + len(extra)),
        out_specs=IN_VMEM,
        scratch_shapes=scratch,
        input_output_aliases={2 + count: 0} if in_place else {},
        compiler_params=pltpu.CompilerParams(vmem_limit_bytes=34 * 2**20),
        cost_estimate=pl.CostEstimate(flops=1000, bytes_accessed=1000, transcendentals=0),
    )(blocks, s_matrix, *pieces, *extra)


def take(which, blocks, s_matrix, depth):
    rows = s_matrix.shape[1]

    def kernel(blocks_ref, s_ref, out_ref, done):
        copies = []
        for k, w in enumerate(which):
            start = pl.multiple_of(blocks_ref[w] * depth, depth)
            copies.append(pltpu.make_async_copy(s_ref.at[:, :, pl.ds(start, depth)], out_ref.at[k], done.at[k]))
        for copy in copies:
            copy.start()
        for copy in copies:
            copy.wait()

    return pl.pallas_call(
        kernel,
        out_shape=jax.ShapeDtypeStruct((len(which), 2, rows, depth), s_matrix.dtype),
        in_specs=[pl.BlockSpec(memory_space=pltpu.SMEM), pl.BlockSpec(memory_space=pltpu.HBM)],
        out_specs=IN_VMEM,
        scratch_shapes=[pltpu.SemaphoreType.DMA((len(which),))],
        compiler_params=pltpu.CompilerParams(vmem_limit_bytes=34 * 2**20),
        cost_estimate=pl.CostEstimate(flops=1000, bytes_accessed=1000, transcendentals=0),
    )(blocks, s_matrix)


def multiply_tiles(which, tiles, pieces, total, finish, received):
    count = len(pieces)
    width, depth = pieces[0].shape
    rows = tiles.shape[2]
    half = width // 2
    extra = [v for v in (total, received) if v is not None]

    def kernel(tiles_ref, *refs):
        total_ref = refs[count]
        received_ref = refs[count + 1] if received is not None else None
        out_ref = refs[count + len(extra)]
        sums = []
        for part in range(2):
            lanes = slice(part * rows, (part + 1) * rows)
            value = total_ref[:, lanes]
            for p in range(count):
                value += lax.dot_general(
                    refs[p][...], tiles_ref[which[p], part], (((1,), (1,)), ((), ())), preferred_element_type=jnp.float32
                )
            if finish:
                sums.append(value)
            else:
                out_ref[:, lanes] = value
        if finish:
            real = sums[0][:half] - sums[1][half:]
            imag = sums[0][half:] + sums[1][:half]
            if received is not None:
                real += received_ref[0].astype(jnp.float32)
                imag += received_ref[1].astype(jnp.float32)
            out_ref[0] = real.astype(out_ref.dtype)
            out_ref[1] = imag.astype(out_ref.dtype)

    out_shape = (
        jax.ShapeDtypeStruct((2, half, rows), jnp.bfloat16)
        if finish
        else jax.ShapeDtypeStruct((width, 2 * rows), jnp.float32)
    )
    return pl.pallas_call(
        kernel,
        out_shape=out_shape,
        in_specs=[IN_VMEM] * (1 + count + len(extra)),
        out_specs=IN_VMEM,
        input_output_aliases={} if finish else {1 + count: 0},
        compiler_params=pltpu.CompilerParams(vmem_limit_bytes=34 * 2**20),
        cost_estimate=pl.CostEstimate(flops=1000, bytes_accessed=1000, transcendentals=0),
    )(tiles, *pieces, *extra)


def choose(flag, first, second, row=0):
    rows = second.shape[0]

    def kernel(flag_ref, first_ref, second_ref, out_ref, done):
        del second_ref

        @pl.when(flag_ref[0] == 1)
        def _():
            copy = pltpu.make_async_copy(first_ref.at[row : row + rows, :], out_ref, done)
            copy.start()
            copy.wait()

    return pl.pallas_call(
        kernel,
        out_shape=jax.ShapeDtypeStruct(second.shape, second.dtype),
        in_specs=[pl.BlockSpec(memory_space=pltpu.SMEM)] + [pl.BlockSpec(memory_space=pl.ANY)] * 2,
        out_specs=pl.BlockSpec(memory_space=pl.ANY),
        scratch_shapes=[pltpu.SemaphoreType.DMA],
        input_output_aliases={2: 0},
        compiler_params=pltpu.CompilerParams(vmem_limit_bytes=34 * 2**20),
        cost_estimate=pl.CostEstimate(flops=1000, bytes_accessed=1000, transcendentals=0),
    )(flag, first, second)


def stack(*parts):
    offsets = [sum(v.shape[0] for v in parts[:k]) for k in range(len(parts))]

    def kernel(*refs):
        out_ref, done = refs[len(parts) :]
        copies = [
            pltpu.make_async_copy(refs[k], out_ref.at[offsets[k] : offsets[k] + v.shape[0], :], done.at[k])
            for k, v in enumerate(parts)
        ]
        for copy in copies:
            copy.start()
        for copy in copies:
            copy.wait()

    return pl.pallas_call(
        kernel,
        out_shape=jax.ShapeDtypeStruct((sum(v.shape[0] for v in parts), parts[0].shape[1]), parts[0].dtype),
        in_specs=[pl.BlockSpec(memory_space=pl.ANY)] * len(parts),
        out_specs=pl.BlockSpec(memory_space=pl.ANY),
        scratch_shapes=[pltpu.SemaphoreType.DMA((len(parts),))],
        compiler_params=pltpu.CompilerParams(vmem_limit_bytes=34 * 2**20),
        cost_estimate=pl.CostEstimate(flops=1000, bytes_accessed=1000, transcendentals=0),
    )(*parts)


def line_of_four(s_matrix, slab, beam_hkl):
    n_row = lax.axis_size("row")
    every = [(z, x, c) for z in range(n_row // PER_PLANE) for x in range(2) for c in range(2)]

    def index(z, x, c):
        return (z * 2 + x) * 2 + c

    def pairs(target, planes=(0, 1, 2, 3)):
        return [(index(*at), index(*target(*at))) for at in every if at[0] in planes]

    across = pairs(lambda z, x, c: (z, 1 - x, c))
    sibling = pairs(lambda z, x, c: (z, x, 1 - c))
    outer = pairs(lambda z, x, c: (z ^ 1, x, c))
    middle = pairs(lambda z, x, c: (3 - z, x, c), (1, 2))
    outward = pairs(lambda z, x, c: (z ^ 1, x, c), (1, 2))

    def send(value, route, what):
        with jax.named_scope("L_" + what):
            return lax.ppermute(value, "row", route)

    def far1(z):
        return 3 - z if z in (1, 2) else z ^ 2

    def far2(z):
        return z ^ 2 if z in (1, 2) else 3 - z

    me = lax.axis_index("row")
    held = {"O": lambda z: z, "P": lambda z: z ^ 1, "M": far1, "N": far2}
    names = [x + c + o for x in ("", "x") for c in ("", "c") for o in held]
    table = [
        [index(held[n[-1]](z), 1 - x if "x" in n else x, 1 - c if "c" in n else c) for n in names]
        + [int(z in (1, 2))]
        for z, x, c in every
    ]
    here = jnp.asarray(np.array(table, np.int32))[me]

    in_middle = here[len(names) :]
    O, Oa, Ob = phase_panels(slab, beam_hkl)
    wide = Oa.shape[0]

    def a(v):
        return (v, 0, wide)

    def b(v):
        return (v, wide, wide)

    def X(v, n):
        return send(v, across, "X" + n)

    def C(v, n):
        return send(v, sibling, "C" + n)

    def mul(which, pieces, total, **kw):
        return multiply([names.index(n) for n in which], here, s_matrix, pieces, total, **kw)

    ob = lax.optimization_barrier

    def upper(v):
        return (v, 0, v.shape[0] // 2)

    def lower(v):
        return (v, v.shape[0] // 2, v.shape[0] // 2)

    CO = C(O, "O")
    XO, Pa, Qa, Pb, Qb = (
        X(O, "O"), send(Oa, outer, "Pa"), send(Oa, middle, "Qa"), send(Ob, outer, "Pb"), send(Ob, middle, "Qb")
    )
    AB = mul(["O", "cO"], [O, CO], None)
    Pa, Qa = ob((Pa, Qa))
    Sa, Ta = send(Qa, outward, "Sa"), send(Pa, middle, "Ta")
    Pa, Pb, Qb, XO, AB = ob((Pa, Pb, Qb, XO, AB))
    XPa, Sb = X(Pa, "Pa"), send(Qb, outward, "Sb")
    CXO = C(XO, "XO")
    P = stack(Pa, Pb)
    AB = mul(["P", "xO"], [P, XO], AB)
    Sa, Ta, XPa, AB = ob((Sa, Ta, XPa, AB))
    M1a = choose(in_middle, Qa, Sa)
    XM1a = X(M1a, "M1a")
    Tb, Ua = send(after(Pb, Sa), middle, "Tb"), send(Ta, outward, "Ua")
    H = C(stack(XPa, M1a), "XPaM1a")
    AB = mul(["xcO"], [CXO], AB)
    A = mul(["xP", "M"], [XPa, M1a], a(AB))
    Sb, XM1a, A, AB = ob((Sb, XM1a, A, AB))
    M1b = choose(in_middle, Qb, Sb)
    XM1b = X(M1b, "M1b")
    Ub = send(Tb, outward, "Ub")
    CXM1a, CM1b = C(XM1a, "XM1a"), C(M1b, "M1b")
    A = mul(["xcP", "cM", "xM"], [upper(H), lower(H), XM1a], A)
    tiles = take([names.index(n) for n in ("xN", "xP", "xcN", "xcP")], after(here, A), s_matrix, O.shape[1])
    Ua, XM1b, XO, A = ob((Ua, XM1b, XO, A))
    M2a = choose(in_middle, Ta, Ua)
    XM2a = X(M2a, "M2a")
    E = send(XO[wide:], outer, "E")
    CXM1b, CM2a = C(XM1b, "XM1b"), C(M2a, "M2a")
    CPa = C(after(Pa, M2a), "Pa")
    B = mul(["M", "cM", "xM"], [M1b, CM1b, XM1b], b(AB))
    Ub, A, B, tiles = ob((Ub, A, B, tiles))
    M2b = choose(in_middle, Tb, Ub)
    XM2b = X(M2b, "M2b")
    XM2a, M2b = ob((XM2a, M2b))
    CXM2a, CM2b = C(XM2a, "XM2a"), C(M2b, "M2b")
    CPb = C(after(Pb, M2b), "Pb")
    partial = mul(["N", "xcM", "cN", "cP", "xN", "xcN"], [M2a, CXM1a, CM2a, CPa, XM2a, CXM2a], A, finish=True)
    with jax.named_scope("L_partial"):
        received = lax.ppermute(partial, "col", [(0, 1), (1, 0)])
    B = mul(["xcM", "cP", "N", "cN"], [CXM1b, CPb, M2b, CM2b], B)
    XM2b, E, B, received, tiles = ob((XM2b, E, B, received, tiles))
    CXM2b, CE = C(XM2b, "XM2b"), C(E, "E")
    B = multiply_tiles([0, 1], tiles, [XM2b, E], B, False, None)
    out = multiply_tiles([2, 3], tiles, [CXM2b, CE], B, True, received)
    return jnp.swapaxes(out, 1, 2)


def any_mesh(s_matrix, slab, beam_hkl):
    real, imag = apply_phase(slab, beam_hkl)
    gathered = lax.all_gather(jnp.stack([real, imag]), "row", axis=2, tiled=True)

    def dot(s, x):
        return lax.dot_general(x, s, (((1,), (1,)), ((), ())), preferred_element_type=jnp.float32)

    part_real = dot(s_matrix[0], gathered[0]) - dot(s_matrix[1], gathered[1])
    part_imag = dot(s_matrix[0], gathered[1]) + dot(s_matrix[1], gathered[0])
    totals = jnp.stack([part_real, part_imag]).astype(jnp.bfloat16)
    return jnp.swapaxes(lax.psum_scatter(totals, "col", scatter_dimension=1, tiled=True), 1, 2)


def solution(mesh):
    placed = (P(None, "row", "col"), P(None, ("col", "row"), None), P(None, ("col", "row")))
    line = mesh.shape["row"] == 4 * PER_PLANE and mesh.shape["col"] == 2
    return jax.shard_map(
        line_of_four if line else any_mesh,
        mesh=mesh,
        in_specs=placed,
        out_specs=P(None, "row", "col"),
        check_vma=False,
    )
```
